32 devices in a mesh: tensor: 4 (over x, core), req: 8 (over z, y).
Axes of the slice: x: 2, y: 2, z: 4, core: 2. Of those that a mesh axis runs over, the one named last changes fastest.
Arguments:
- attention_output: bfloat16 [4096, 4096], P('req', 'tensor'), may hold values from -6 to 6
- residual: bfloat16 [4096, 8192], P('req', 'tensor'), may hold values from -6 to 6
- projection_weight: bfloat16 [4096, 8192], P('tensor'), may hold values from -0.09375 to 0.09375
- adapter_down_maps: bfloat16 [64, 4096, 64], P('req', 'tensor'), may hold values from -0.09375 to 0.09375
- adapter_up_maps: bfloat16 [64, 64, 8192], P('req', None, 'tensor'), may hold values from -0.75 to 0.75
- adapter_pool_slot: int32 [64], replicated, may hold values from 0 to 63, as said below
- request_adapter_id: int32 [8, 8], replicated, may hold values from 0 to 63, as said below
- request_token_length: int32 [8, 8], P('req'), may hold values from 1 to 128, 512 in all within a row
Outputs:
- mixed: bfloat16 [4096, 8192], P('req', 'tensor')
The draws below stay inside these ranges and needn't reach their ends.
Inputs may be any that keep to these rules, and one draw needn't show every extreme that they name: `adapter_pool_slot`: each slot appears once; the slot s lies on index s // 8 of req, its owner. `request_adapter_id`: the 8 requests of one group use adapters with 8 distinct owners. `request_token_length`: each group's lengths sum to 512; in each group the largest is exactly 128.
All inputs are finite; a program needn't handle non-finite values.
Results may differ from the reference program's by a relative error of at most 0.014.
Values may be sent and summed in bfloat16 or wider, within the bound.
A program may use at most 128 MiB of HBM per device.

```python
import math
import jax
import jax.numpy as jnp
import numpy as np
from jax import lax

MODEL_WIDTH = 8192
ADAPTER_RANK = 64
TOK_DEV = 512
ADAPT_DEV = 8
ATTENTION_WIDTH = 4096
GROUPS = 8
REQ_GRP = 8
MOST = 128
ADAPTER_POOL = 64
TOKENS = 4096
N_TENSOR = 4


def pick_adapters(key):
    base_key = jax.random.fold_in(key, 7)
    slot_key, heat_key, pick_key, row_key = jax.random.split(base_key, 4)
    request_slots = jax.random.permutation(slot_key, ADAPTER_POOL).astype(jnp.int32)
    heat = jax.random.randint(heat_key, (GROUPS,), 0, 3 * GROUPS)
    noise = jax.random.randint(pick_key, (GROUPS, GROUPS), 0, 2 * GROUPS)
    scores = (heat[None, :] + noise) * GROUPS + jnp.arange(GROUPS, dtype=jnp.int32)[None, :]
    owners = lax.top_k(scores.astype(jnp.int32), REQ_GRP)[1].astype(jnp.int32)
    local = jax.random.randint(row_key, (GROUPS, REQ_GRP), 0, ADAPT_DEV).astype(jnp.int32)
    wanted = owners * ADAPT_DEV + local
    inverse = jnp.argsort(request_slots).astype(jnp.int32)
    return (request_slots, jnp.take(inverse, wanted).astype(jnp.int32))


def draw_adapter_pool_slot(key, part):
    return pick_adapters(key)[0]


def draw_request_adapter_id(key, part):
    return pick_adapters(key)[1]


def block_scale(stream_key, extent, shards, smallest, top_value):
    loudness = 1.0
    for axis_at, parts in shards:
        steps = jax.random.uniform(jax.random.fold_in(jax.random.fold_in(stream_key, 6), axis_at), (parts,), jnp.float32, smallest / len(shards), top_value / len(shards))
        loudness = loudness * jnp.repeat(jnp.exp(steps), extent[axis_at] // parts).reshape((-1,) + (1,) * (len(extent) - 1 - axis_at))
    return loudness


def split_up(count, total, reach, slope):
    weights = [(1 << 20) // math.isqrt(grade ** slope) + 1 for grade in range(2, count + 1)]
    surplus, counts = total - reach - (count - 1), [1] * (count - 1)
    while surplus > 0:
        free = [i for i in range(count - 1) if counts[i] < reach]
        whole, budget = sum([weights[i] for i in free]), surplus
        for i in free:
            extra = min(reach - counts[i], max(1, budget * weights[i] // whole), surplus)
            counts[i] = counts[i] + extra
            surplus = surplus - extra
    return np.array([reach] + counts)


def ragged(stream_key, amount, total, most, skew):
    if amount == 2:
        one = jax.random.randint(stream_key, (), max(1, total - most), min(most, total - 1) + 1)
        return jnp.stack([one, total - one])
    sizes = jnp.asarray(split_up(amount, total, most, skew), jnp.int32)
    pairs = (amount - 1) // 2
    donor, receiver = sizes[1:1 + 2 * pairs:2], sizes[2:2 + 2 * pairs:2]
    margin = jnp.minimum(donor - 1, most - receiver)
    passed = jax.random.randint(jax.random.fold_in(stream_key, 1), (pairs,), 0, 1 << 20) % (margin + 1)
    sizes = sizes.at[1:1 + 2 * pairs:2].set(donor - passed).at[2:2 + 2 * pairs:2].set(receiver + passed)
    return sizes[jax.random.permutation(jax.random.fold_in(stream_key, 2), amount)]


def bell_draw(stream_key, shape, scale, limit, pieces=(), held_as=jnp.bfloat16):
    array = jax.random.normal(stream_key, shape, jnp.float32) * scale
    if len(pieces) > 0:
        array = block_scale(stream_key, shape, pieces, -0.22, 0.18) * array
    return jnp.clip(array, min=-limit, max=limit).astype(held_as)


def setup_inputs(seed: int = 0) -> dict:
    seeds = jax.random.split(jax.random.key(seed), 9)
    return {
        "attention_output": bell_draw(seeds[0], (TOKENS, ATTENTION_WIDTH), 1.0, 6.0, ((0, 8), (1, 4))),
        "residual": bell_draw(seeds[1], (TOKENS, MODEL_WIDTH), 1.0, 6.0, ((0, 8), (1, 4))),
        "projection_weight": bell_draw(seeds[2], (ATTENTION_WIDTH, MODEL_WIDTH), ATTENTION_WIDTH ** -0.5, 0.09375, ((0, 4),)),
        "adapter_down_maps": bell_draw(seeds[3], (ADAPTER_POOL, ATTENTION_WIDTH, ADAPTER_RANK), ATTENTION_WIDTH ** -0.5, 0.09375, ((0, 8), (1, 4))),
        "adapter_up_maps": bell_draw(seeds[4], (ADAPTER_POOL, ADAPTER_RANK, MODEL_WIDTH), ADAPTER_RANK ** -0.5, 0.75, ((0, 8), (2, 4))),
        "adapter_pool_slot": draw_adapter_pool_slot(jax.random.fold_in(seeds[8], 71), 0),
        "request_adapter_id": draw_request_adapter_id(jax.random.fold_in(seeds[8], 71), 0),
        "request_token_length": jax.vmap(lambda own: ragged(own, REQ_GRP, TOK_DEV, MOST, 2))(jax.random.split(seeds[7], GROUPS)).reshape((GROUPS, REQ_GRP)).astype(jnp.int32),
    }


def reference(attention_output, residual, projection_weight, adapter_down_maps, adapter_up_maps, adapter_pool_slot, request_adapter_id, request_token_length):
    width = ATTENTION_WIDTH // N_TENSOR

    def one_group(group):
        rows = lax.dynamic_slice_in_dim(attention_output, group * TOK_DEV, TOK_DEV, 0)
        stream = lax.dynamic_slice_in_dim(residual, group * TOK_DEV, TOK_DEV, 0)
        base = jnp.zeros((TOK_DEV, MODEL_WIDTH), jnp.float32)
        for shard in range(N_TENSOR):
            part = jnp.dot(rows[:, shard * width:(shard + 1) * width], projection_weight[shard * width:(shard + 1) * width], preferred_element_type=jnp.float32)
            base = base + part.astype(jnp.bfloat16).astype(jnp.float32)
        request_slots = jnp.take(adapter_pool_slot, request_adapter_id[group])
        lengths = request_token_length[group]
        ends = jnp.cumsum(lengths)
        starts = (ends - lengths).astype(jnp.int32)
        padded = jnp.concatenate([rows, jnp.zeros((MOST, ATTENTION_WIDTH), rows.dtype)], 0)
        delta = jnp.zeros((TOK_DEV + MOST, MODEL_WIDTH), jnp.float32)
        inside = jnp.arange(MOST, dtype=jnp.int32)
        for request_number in range(REQ_GRP):
            start = starts[request_number].astype(jnp.int32)
            request_span = lax.dynamic_slice_in_dim(padded, start, MOST, 0)
            token_mask = (inside < lengths[request_number]).astype(jnp.float32)[:, None]
            reduced_rows = (token_mask * jnp.dot(request_span, adapter_down_maps[request_slots[request_number]], preferred_element_type=jnp.float32)).astype(jnp.bfloat16)
            raised_output = token_mask * jnp.dot(reduced_rows, adapter_up_maps[request_slots[request_number]], preferred_element_type=jnp.float32)
            current = lax.dynamic_slice_in_dim(delta, start, MOST, 0)
            delta = lax.dynamic_update_slice_in_dim(delta, current + raised_output, start, 0)
        return (stream.astype(jnp.float32) + base + delta[:TOK_DEV]).astype(jnp.bfloat16)

    blocks = lax.map(one_group, jnp.arange(GROUPS, dtype=jnp.int32))
    return blocks.reshape(TOKENS, MODEL_WIDTH)
```

```python
import functools

import jax
import jax.numpy as jnp
from jax import lax
from jax.experimental import pallas as pl
from jax.experimental.pallas import tpu as pltpu
from jax.sharding import PartitionSpec as P

MESH = pl.DeviceIdType.MESH
BF16 = jnp.bfloat16
F32 = jnp.float32


def select_kernel(rows_ref, down_ref, up_ref, down_out, up_out):
    del rows_ref
    down_out[0] = down_ref[0]
    up_out[0] = up_ref[0]


def select(block_rows, down_maps, up_maps):
    groups = block_rows.shape[0]
    _, rank, depth = down_maps.shape
    width = up_maps.shape[2]
    return pl.pallas_call(
        select_kernel,
        grid_spec=pltpu.PrefetchScalarGridSpec(
            num_scalar_prefetch=1,
            grid=(groups,),
            in_specs=[
                pl.BlockSpec((1, rank, depth), lambda g, rows: (rows[g], 0, 0)),
                pl.BlockSpec((1, rank, width), lambda g, rows: (rows[g], 0, 0)),
            ],
            out_specs=[
                pl.BlockSpec((1, rank, depth), lambda g, rows: (g, 0, 0)),
                pl.BlockSpec((1, rank, width), lambda g, rows: (g, 0, 0)),
            ],
        ),
        out_shape=[
            jax.ShapeDtypeStruct((groups, rank, depth), BF16),
            jax.ShapeDtypeStruct((groups, rank, width), BF16),
        ],
        name="select_adapters",
    )(block_rows, down_maps, up_maps)


def kernel(
    groups, tensor, tile,
    x_ref, w_hbm, res_ref, owner_ref, down_hbm, up_hbm, out_ref,
    w_ref, pair_out, pair_in, chip_out, chip_in, base, down_in, up_in, low_out, low_in, lows,
    w_sem, own_sem, down_send, down_recv, up_send, up_recv,
    pair_send, pair_recv, chip_send, chip_recv, low_send, low_recv,
):
    me_t, me_r = lax.axis_index("tensor"), lax.axis_index("req")
    chips = tensor // 2
    chip, core = me_t // 2, lax.rem(me_t, 2)
    partner = chip * 2 + 1 - core
    width = out_ref.shape[1]
    tiles = width // tile
    rank = up_in.shape[1]
    blocks = []
    for step in range(1, chips + 1):
        there = lax.rem(chip + step, chips)
        blocks += [there * 2 + 1 - core, there * 2 + core]

    def weight_copy(i):
        column = pl.multiple_of(blocks[i] * width, width)
        return pltpu.make_async_copy(w_hbm.at[:, pl.ds(column, width)], w_ref.at[i], w_sem.at[i])

    def down_copy(peer, slot):
        return pltpu.make_async_remote_copy(
            src_ref=down_hbm.at[peer], dst_ref=down_in.at[slot],
            send_sem=down_send.at[peer], recv_sem=down_recv.at[slot],
            device_id=(me_t, peer), device_id_type=MESH)

    def up_copy(peer, slot):
        return pltpu.make_async_remote_copy(
            src_ref=up_hbm.at[peer], dst_ref=up_in.at[slot],
            send_sem=up_send.at[peer], recv_sem=up_recv.at[slot],
            device_id=(me_t, peer), device_id_type=MESH)

    def pair_copy(step, q):
        return pltpu.make_async_remote_copy(
            src_ref=pair_out.at[step, q], dst_ref=pair_in.at[step, q],
            send_sem=pair_send.at[step, q], recv_sem=pair_recv.at[step, q],
            device_id=(partner, me_r), device_id_type=MESH)

    def chip_copy(step, q):
        there = lax.rem(chip + step + 1, chips)
        return pltpu.make_async_remote_copy(
            src_ref=chip_out.at[step, q], dst_ref=chip_in.at[step, q],
            send_sem=chip_send.at[step, q], recv_sem=chip_recv.at[step, q],
            device_id=(there * 2 + core, me_r), device_id_type=MESH)

    def low_copy(step):
        return pltpu.make_async_remote_copy(
            src_ref=low_out, dst_ref=low_in.at[step - 1],
            send_sem=low_send.at[step - 1], recv_sem=low_recv.at[step - 1],
            device_id=(lax.rem(me_t + step, tensor), me_r), device_id_type=MESH)

    for i in range(2 * chips):
        weight_copy(i).start()
    own_down = pltpu.make_async_copy(down_hbm.at[me_r], down_in.at[me_r], own_sem.at[0])
    own_up = pltpu.make_async_copy(up_hbm.at[me_r], up_in.at[me_r], own_sem.at[1])

    barrier = pltpu.get_barrier_semaphore()

    @pl.loop(1, groups)
    def _(d):
        pl.semaphore_signal(
            barrier, inc=1, device_id=(me_t, lax.rem(me_r + d, groups)), device_id_type=MESH)

    for d in range(1, tensor):
        pl.semaphore_signal(
            barrier, inc=1, device_id=(lax.rem(me_t + d, tensor), me_r), device_id_type=MESH)
    pl.semaphore_wait(barrier, groups - 1 + tensor - 1)

    @pl.loop(1, groups)
    def _(d):
        down_copy(lax.rem(me_r + d, groups), me_r).start()

    @pl.loop(1, groups)
    def _(d):
        up_copy(lax.rem(me_r + d, groups), me_r).start()

    own_down.start()
    own_up.start()

    def product(i, q):
        columns = pl.ds(pl.multiple_of(q * tile, tile), tile)
        return jnp.dot(x_ref[...], w_ref[i, :, columns], preferred_element_type=F32)

    for step in range(chips):
        weight_copy(2 * step).wait()

        @pl.loop(0, tiles)
        def _(q):
            pair_out[step, q] = product(2 * step, q).astype(BF16)
            pair_copy(step, q).start()

        weight_copy(2 * step + 1).wait()

        @pl.loop(0, tiles)
        def _(q):
            mine = product(2 * step + 1, q)
            pair_copy(step, q).wait_recv()
            total = mine + pair_in[step, q].astype(F32)
            if step < chips - 1:
                chip_out[step, q] = total.astype(BF16)
                chip_copy(step, q).start()
            else:
                base[q] = total

    own_down.wait()

    @pl.loop(1, groups)
    def _(d):
        peer = lax.rem(me_r + d, groups)
        down_copy(peer, peer).wait_recv()

    span = 2 * rank
    owner = owner_ref[...]
    lane_owner = lax.broadcasted_iota(jnp.int32, (1, span), 1) // rank
    low = jnp.zeros(low_out.shape, F32)
    for pair in range(groups // 2):
        maps = down_in[2 * pair : 2 * pair + 2].reshape(span, x_ref.shape[1])
        value = lax.dot_general(
            x_ref[...], maps, (((1,), (1,)), ((), ())), preferred_element_type=F32)
        low = low + jnp.where(owner == 2 * pair + lane_owner, value, 0.0)
    low_out[...] = low.astype(BF16)
    for step in range(1, tensor):
        low_copy(step).start()
    low = low_out[...].astype(F32)
    for step in range(1, tensor):
        low_copy(step).wait_recv()
        low = low + low_in[step - 1].astype(F32)
    for pair in range(groups // 2):
        lows[:, pair * span : (pair + 1) * span] = jnp.where(
            owner == 2 * pair + lane_owner, low, 0.0).astype(BF16)

    for step in range(chips - 1):
        @pl.loop(0, tiles)
        def _(q):
            chip_copy(step, q).wait_recv()
            base[q] = base[q] + chip_in[step, q].astype(F32)

    own_up.wait()

    @pl.loop(1, groups)
    def _(d):
        peer = lax.rem(me_r + d, groups)
        up_copy(peer, peer).wait_recv()

    @pl.loop(0, tiles)
    def _(q):
        columns = pl.ds(pl.multiple_of(q * tile, tile), tile)
        maps = up_in[:, :, columns].reshape(groups * rank, tile)
        delta = jnp.dot(lows[...], maps, preferred_element_type=F32)
        out_ref[:, columns] = (res_ref[:, columns].astype(F32) + base[q] + delta).astype(BF16)

    @pl.loop(1, groups)
    def _(d):
        peer = lax.rem(me_r + d, groups)
        down_copy(peer, me_r).wait_send()
        up_copy(peer, me_r).wait_send()

    for step in range(chips):
        @pl.loop(0, tiles)
        def _(q):
            pair_copy(step, q).wait_send()
            if step < chips - 1:
                chip_copy(step, q).wait_send()

    for step in range(1, tensor):
        low_copy(step).wait_send()


def per_device(
    attention_output,
    residual,
    projection_weight,
    adapter_down_maps,
    adapter_up_maps,
    adapter_pool_slot,
    request_adapter_id,
    request_token_length,
):
    groups, tensor = lax.axis_size("req"), lax.axis_size("tensor")
    me_index = lax.axis_index("req")
    tokens, depth = attention_output.shape
    width = residual.shape[1]
    pool, _, rank = adapter_down_maps.shape
    lengths = request_token_length[0]
    order = jnp.arange(lengths.shape[0], dtype=jnp.int32)
    ends = jnp.sum(jnp.where(order[None, :] <= order[:, None], lengths[None, :], 0), 1)
    owners = jnp.take(adapter_pool_slot, request_adapter_id) // pool
    slots = jnp.take(adapter_pool_slot, request_adapter_id) % pool
    my_owner = lax.dynamic_index_in_dim(owners, me_index, 0, keepdims=False)
    positions = jnp.arange(tokens, dtype=jnp.int32)
    tok_req = jnp.sum((positions[:, None] >= ends[None, :]).astype(jnp.int32), 1)
    req_hot = tok_req[:, None] == jnp.arange(ends.shape[0], dtype=jnp.int32)[None, :]
    tok_owner = jnp.sum(jnp.where(req_hot, my_owner[None, :], 0), 1, keepdims=True)
    block_rows = jnp.sum(jnp.where(owners == me_index, slots, 0), 1)
    downs, ups = select(block_rows, adapter_down_maps.transpose(0, 2, 1), adapter_up_maps)

    tile = min(512, width)
    tiles = width // tile
    chips = tensor // 2
    far = max(chips - 1, 1)
    vmem = pl.BlockSpec(memory_space=pltpu.VMEM)
    hbm = pl.BlockSpec(memory_space=pl.ANY)
    dma = pltpu.SemaphoreType.DMA
    flops = 2 * tokens * depth * width * tensor
    return pl.pallas_call(
        functools.partial(kernel, groups, tensor, tile),
        out_shape=jax.ShapeDtypeStruct((tokens, width), BF16),
        in_specs=[vmem, hbm, vmem, vmem, hbm, hbm],
        out_specs=vmem,
        scratch_shapes=[
            pltpu.VMEM((tensor, depth, width), BF16),
            pltpu.VMEM((chips, tiles, tokens, tile), BF16),
            pltpu.VMEM((chips, tiles, tokens, tile), BF16),
            pltpu.VMEM((far, tiles, tokens, tile), BF16),
            pltpu.VMEM((far, tiles, tokens, tile), BF16),
            pltpu.VMEM((tiles, tokens, tile), F32),
            pltpu.VMEM((groups, rank, depth), BF16),
            pltpu.VMEM((groups, rank, width), BF16),
            pltpu.VMEM((tokens, 2 * rank), BF16),
            pltpu.VMEM((tensor - 1, tokens, 2 * rank), BF16),
            pltpu.VMEM((tokens, groups * rank), BF16),
            dma((tensor,)),
            dma((2,)),
            dma((groups,)),
            dma((groups,)),
            dma((groups,)),
            dma((groups,)),
            dma((chips, tiles)),
            dma((chips, tiles)),
            dma((far, tiles)),
            dma((far, tiles)),
            dma((tensor - 1,)),
            dma((tensor - 1,)),
        ],
        compiler_params=pltpu.CompilerParams(
            collective_id=0, has_side_effects=True, vmem_limit_bytes=56 * 1024 * 1024
        ),
        cost_estimate=pl.CostEstimate(
            flops=flops, bytes_accessed=2 * depth * width * tensor, transcendentals=0
        ),
        name="project_and_adapt",
    )(attention_output, projection_weight, residual, tok_owner, downs, ups)


def solution(mesh):
    in_specs = (
        P("req", "tensor"),
        P("req", "tensor"),
        P("tensor", None),
        P("req", "tensor", None),
        P("req", None, "tensor"),
        P(),
        P(),
        P("req", None),
    )
    out_specs = P("req", "tensor")
    return jax.shard_map(
        per_device, mesh=mesh, in_specs=in_specs, out_specs=out_specs, check_vma=False
    )
```

```python
import functools

import jax
import jax.numpy as jnp
from jax import lax
from jax.experimental import pallas as pl
from jax.experimental.pallas import tpu as pltpu
from jax.sharding import PartitionSpec as P

MESH = pl.DeviceIdType.MESH
BF16 = jnp.bfloat16
F32 = jnp.float32


def select_kernel(
    slot_ref, id_ref, length_ref, me_ref, down_hbm, up_hbm, down_out, up_out, owner_out, rows, sems
):
    groups, requests = id_ref.shape
    pool = down_hbm.shape[0]
    me = me_ref[0]

    @pl.loop(0, groups)
    def _(g):
        def find(r, row):
            slot = slot_ref[id_ref[g, r]]
            return row + jnp.where(slot // pool == me, slot % pool, 0)

        row = lax.fori_loop(0, requests, find, jnp.int32(0), unroll=True)
        rows[g] = row
        pltpu.make_async_copy(down_hbm.at[row], down_out.at[g], sems.at[0, g]).start()
        pltpu.make_async_copy(up_hbm.at[row], up_out.at[g], sems.at[1, g]).start()

    positions = lax.broadcasted_iota(jnp.int32, owner_out.shape, 0)
    start = jnp.int32(0)
    owner = jnp.zeros(owner_out.shape, jnp.int32)
    for r in range(requests):
        mine = slot_ref[id_ref[me, r]] // pool
        owner = jnp.where(positions >= start, mine, owner)
        start = start + length_ref[0, r]
    owner_out[...] = owner

    @pl.loop(0, groups)
    def _(g):
        row = rows[g]
        pltpu.make_async_copy(down_hbm.at[row], down_out.at[g], sems.at[0, g]).wait()
        pltpu.make_async_copy(up_hbm.at[row], up_out.at[g], sems.at[1, g]).wait()


def select(slots, ids, lengths, me, down_maps, up_maps, tokens):
    groups = ids.shape[0]
    _, rank, depth = down_maps.shape
    width = up_maps.shape[2]
    smem = pl.BlockSpec(memory_space=pltpu.SMEM)
    hbm = pl.BlockSpec(memory_space=pl.ANY)
    return pl.pallas_call(
        select_kernel,
        in_specs=[smem, smem, smem, smem, hbm, hbm],
        out_specs=[hbm, hbm, pl.BlockSpec(memory_space=pltpu.VMEM)],
        out_shape=[
            jax.ShapeDtypeStruct((groups, rank, depth), BF16),
            jax.ShapeDtypeStruct((groups, rank, width), BF16),
            jax.ShapeDtypeStruct((tokens, 2 * rank), jnp.int32),
        ],
        scratch_shapes=[pltpu.SMEM((groups,), jnp.int32), pltpu.SemaphoreType.DMA((2, groups))],
        name="select_adapters",
    )(slots, ids, lengths, me, down_maps, up_maps)


def finish_kernel(low_ref, up_ref, base_ref, out_ref):
    maps = up_ref[...].reshape(low_ref.shape[1], out_ref.shape[1])
    delta = jnp.dot(low_ref[...], maps, preferred_element_type=F32)
    out_ref[...] = (base_ref[0] + delta).astype(BF16)


def finish(lows, ups, base):
    tokens, depth = lows.shape
    groups, rank, width = ups.shape
    tiles, _, tile = base.shape
    return pl.pallas_call(
        finish_kernel,
        grid=(tiles,),
        in_specs=[
            pl.BlockSpec((tokens, depth), lambda q: (0, 0)),
            pl.BlockSpec((groups, rank, tile), lambda q: (0, 0, q)),
            pl.BlockSpec((1, tokens, tile), lambda q: (q, 0, 0)),
        ],
        out_specs=pl.BlockSpec((tokens, tile), lambda q: (0, q)),
        out_shape=jax.ShapeDtypeStruct((tokens, width), BF16),
        compiler_params=pltpu.CompilerParams(vmem_limit_bytes=56 * 1024 * 1024),
        name="raise_and_add",
    )(lows, ups, base)


def kernel(
    groups, tensor, tile,
    x_ref, w_hbm, res_ref, owner_ref, down_hbm, up_hbm, low_hbm, up_in, base_hbm,
    w_ref, pair_out, pair_in, chip_out, chip_in, base, down_in, low_out, low_in, lows,
    w_sem, own_sem, out_sem, down_send, down_recv, up_send, up_recv,
    pair_send, pair_recv, chip_send, chip_recv, low_send, low_recv,
):
    me_t, me_r = lax.axis_index("tensor"), lax.axis_index("req")
    chips = tensor // 2
    chip, core = me_t // 2, lax.rem(me_t, 2)
    partner = chip * 2 + 1 - core
    width = res_ref.shape[1]
    tiles = width // tile
    rank = up_in.shape[1]
    blocks = []
    for step in range(1, chips + 1):
        there = lax.rem(chip + step, chips)
        blocks += [there * 2 + 1 - core, there * 2 + core]

    def far_first(k):
        half = (k + 1) // 2
        return lax.rem(me_r + groups // 2 + half - 2 * half * lax.rem(k, 2), groups)

    def weight_copy(i):
        column = pl.multiple_of(blocks[i] * width, width)
        return pltpu.make_async_copy(w_hbm.at[:, pl.ds(column, width)], w_ref.at[i], w_sem.at[i])

    def down_copy(peer, slot):
        return pltpu.make_async_remote_copy(
            src_ref=down_hbm.at[peer], dst_ref=down_in.at[slot],
            send_sem=down_send.at[peer], recv_sem=down_recv.at[slot],
            device_id=(me_t, peer), device_id_type=MESH)

    def up_copy(peer, slot):
        return pltpu.make_async_remote_copy(
            src_ref=up_hbm.at[peer], dst_ref=up_in.at[slot],
            send_sem=up_send.at[peer], recv_sem=up_recv.at[slot],
            device_id=(me_t, peer), device_id_type=MESH)

    def pair_copy(step, q):
        return pltpu.make_async_remote_copy(
            src_ref=pair_out.at[step, q], dst_ref=pair_in.at[step, q],
            send_sem=pair_send.at[step, q], recv_sem=pair_recv.at[step, q],
            device_id=(partner, me_r), device_id_type=MESH)

    def chip_copy(step, q):
        there = lax.rem(chip + step + 1, chips)
        return pltpu.make_async_remote_copy(
            src_ref=chip_out.at[step, q], dst_ref=chip_in.at[step, q],
            send_sem=chip_send.at[step, q], recv_sem=chip_recv.at[step, q],
            device_id=(there * 2 + core, me_r), device_id_type=MESH)

    def low_copy(step):
        return pltpu.make_async_remote_copy(
            src_ref=low_out, dst_ref=low_in.at[step - 1],
            send_sem=low_send.at[step - 1], recv_sem=low_recv.at[step - 1],
            device_id=(lax.rem(me_t + step, tensor), me_r), device_id_type=MESH)

    for i in range(2 * chips):
        weight_copy(i).start()
    own_down = pltpu.make_async_copy(down_hbm.at[me_r], down_in.at[me_r], own_sem.at[0])
    own_up = pltpu.make_async_copy(up_hbm.at[me_r], up_in.at[me_r], own_sem.at[1])

    barrier = pltpu.get_barrier_semaphore()

    @pl.loop(1, groups)
    def _(d):
        pl.semaphore_signal(
            barrier, inc=1, device_id=(me_t, lax.rem(me_r + d, groups)), device_id_type=MESH)

    for d in range(1, tensor):
        pl.semaphore_signal(
            barrier, inc=1, device_id=(lax.rem(me_t + d, tensor), me_r), device_id_type=MESH)
    pl.semaphore_wait(barrier, groups - 1 + tensor - 1)

    @pl.loop(0, groups - 1)
    def _(k):
        down_copy(far_first(k), me_r).start()

    @pl.loop(0, groups - 1)
    def _(k):
        up_copy(far_first(k), me_r).start()

    own_down.start()
    own_up.start()

    def product(i, q):
        columns = pl.ds(pl.multiple_of(q * tile, tile), tile)
        return jnp.dot(x_ref[...], w_ref[i, :, columns], preferred_element_type=F32)

    for step in range(chips):
        weight_copy(2 * step).wait()

        @pl.loop(0, tiles)
        def _(q):
            pair_out[step, q] = product(2 * step, q).astype(BF16)
            pair_copy(step, q).start()

        weight_copy(2 * step + 1).wait()

        @pl.loop(0, tiles)
        def _(q):
            mine = product(2 * step + 1, q)
            pair_copy(step, q).wait_recv()
            total = mine + pair_in[step, q].astype(F32)
            if step < chips - 1:
                chip_out[step, q] = total.astype(BF16)
                chip_copy(step, q).start()
            else:
                base[q] = total

    own_down.wait()

    @pl.loop(1, groups)
    def _(d):
        peer = lax.rem(me_r + d, groups)
        down_copy(peer, peer).wait_recv()

    span = 2 * rank
    owner = owner_ref[...]
    lane_owner = lax.broadcasted_iota(jnp.int32, (1, span), 1) // rank
    low = jnp.zeros(low_out.shape, F32)
    for pair in range(groups // 2):
        maps = down_in[2 * pair : 2 * pair + 2].reshape(span, x_ref.shape[1])
        value = lax.dot_general(
            x_ref[...], maps, (((1,), (1,)), ((), ())), preferred_element_type=F32)
        low = low + jnp.where(owner == 2 * pair + lane_owner, value, 0.0)
    low_out[...] = low.astype(BF16)
    for step in range(1, tensor):
        low_copy(step).start()
    low = low_out[...].astype(F32)
    for step in range(1, tensor):
        low_copy(step).wait_recv()
        low = low + low_in[step - 1].astype(F32)
    for pair in range(groups // 2):
        lows[:, pair * span : (pair + 1) * span] = jnp.where(
            owner == 2 * pair + lane_owner, low, 0.0).astype(BF16)
    low_write = pltpu.make_async_copy(lows, low_hbm, own_sem.at[2])
    low_write.start()

    def base_write(q):
        return pltpu.make_async_copy(base.at[q], base_hbm.at[q], out_sem.at[q])

    @pl.loop(0, tiles)
    def _(q):
        columns = pl.ds(pl.multiple_of(q * tile, tile), tile)
        total = base[q] + res_ref[:, columns].astype(F32)
        for step in range(chips - 1):
            chip_copy(step, q).wait_recv()
            total = total + chip_in[step, q].astype(F32)
        base[q] = total
        base_write(q).start()

    own_up.wait()

    @pl.loop(1, groups)
    def _(d):
        peer = lax.rem(me_r + d, groups)
        up_copy(peer, peer).wait_recv()

    low_write.wait()

    @pl.loop(0, tiles)
    def _(q):
        base_write(q).wait()

    @pl.loop(1, groups)
    def _(d):
        peer = lax.rem(me_r + d, groups)
        down_copy(peer, me_r).wait_send()
        up_copy(peer, me_r).wait_send()

    for step in range(chips):
        @pl.loop(0, tiles)
        def _(q):
            pair_copy(step, q).wait_send()
            if step < chips - 1:
                chip_copy(step, q).wait_send()

    for step in range(1, tensor):
        low_copy(step).wait_send()


def per_device(
    attention_output,
    residual,
    projection_weight,
    adapter_down_maps,
    adapter_up_maps,
    adapter_pool_slot,
    request_adapter_id,
    request_token_length,
):
    groups, tensor = lax.axis_size("req"), lax.axis_size("tensor")
    me_index = lax.axis_index("req")
    tokens, depth = attention_output.shape
    width = residual.shape[1]
    rank = adapter_down_maps.shape[2]
    me = jnp.reshape(me_index, (1,))
    downs, ups, owner = select(
        adapter_pool_slot, request_adapter_id, request_token_length, me,
        adapter_down_maps.transpose(0, 2, 1), adapter_up_maps, tokens)

    tile = min(512, width)
    tiles = width // tile
    chips = tensor // 2
    far = max(chips - 1, 1)
    vmem = pl.BlockSpec(memory_space=pltpu.VMEM)
    hbm = pl.BlockSpec(memory_space=pl.ANY)
    dma = pltpu.SemaphoreType.DMA
    flops = 2 * tokens * depth * width * tensor
    lows, ups, base = pl.pallas_call(
        functools.partial(kernel, groups, tensor, tile),
        out_shape=[
            jax.ShapeDtypeStruct((tokens, groups * rank), BF16),
            jax.ShapeDtypeStruct((groups, rank, width), BF16),
            jax.ShapeDtypeStruct((tiles, tokens, tile), F32),
        ],
        in_specs=[vmem, hbm, vmem, vmem, hbm, hbm],
        out_specs=[hbm, hbm, hbm],
        scratch_shapes=[
            pltpu.VMEM((tensor, depth, width), BF16),
            pltpu.VMEM((chips, tiles, tokens, tile), BF16),
            pltpu.VMEM((chips, tiles, tokens, tile), BF16),
            pltpu.VMEM((far, tiles, tokens, tile), BF16),
            pltpu.VMEM((far, tiles, tokens, tile), BF16),
            pltpu.VMEM((tiles, tokens, tile), F32),
            pltpu.VMEM((groups, rank, depth), BF16),
            pltpu.VMEM((tokens, 2 * rank), BF16),
            pltpu.VMEM((tensor - 1, tokens, 2 * rank), BF16),
            pltpu.VMEM((tokens, groups * rank), BF16),
            dma((tensor,)),
            dma((3,)),
            dma((tiles,)),
            dma((groups,)),
            dma((groups,)),
            dma((groups,)),
            dma((groups,)),
            dma((chips, tiles)),
            dma((chips, tiles)),
            dma((far, tiles)),
            dma((far, tiles)),
            dma((tensor - 1,)),
            dma((tensor - 1,)),
        ],
        compiler_params=pltpu.CompilerParams(
            collective_id=0, has_side_effects=True, vmem_limit_bytes=56 * 1024 * 1024
        ),
        cost_estimate=pl.CostEstimate(
            flops=flops, bytes_accessed=2 * depth * width * tensor, transcendentals=0
        ),
        name="project_and_adapt",
    )(attention_output, projection_weight, residual, owner, downs, ups)
    return finish(lows, ups, base)


def solution(mesh):
    in_specs = (
        P("req", "tensor"),
        P("req", "tensor"),
        P("tensor", None),
        P("req", "tensor", None),
        P("req", None, "tensor"),
        P(),
        P(),
        P("req", None),
    )
    out_specs = P("req", "tensor")
    return jax.shard_map(
        per_device, mesh=mesh, in_specs=in_specs, out_specs=out_specs, check_vma=False
    )
```

```python
import functools

import jax
import jax.numpy as jnp
from jax import lax
from jax.experimental import pallas as pl
from jax.experimental.pallas import tpu as pltpu
from jax.sharding import PartitionSpec as P

MESH = pl.DeviceIdType.MESH
BF16 = jnp.bfloat16
F32 = jnp.float32


def finish_kernel(low_ref, up_ref, base_ref, out_ref):
    maps = up_ref[...].reshape(low_ref.shape[1], out_ref.shape[1])
    delta = jnp.dot(low_ref[...], maps, preferred_element_type=F32)
    out_ref[...] = (base_ref[0] + delta).astype(BF16)


def finish(lows, ups, base):
    tokens, depth = lows.shape
    groups, rank, width = ups.shape
    tiles, _, tile = base.shape
    return pl.pallas_call(
        finish_kernel,
        grid=(tiles,),
        in_specs=[
            pl.BlockSpec((tokens, depth), lambda q: (0, 0)),
            pl.BlockSpec((groups, rank, tile), lambda q: (0, 0, q)),
            pl.BlockSpec((1, tokens, tile), lambda q: (q, 0, 0)),
        ],
        out_specs=pl.BlockSpec((tokens, tile), lambda q: (0, q)),
        out_shape=jax.ShapeDtypeStruct((tokens, width), BF16),
        compiler_params=pltpu.CompilerParams(vmem_limit_bytes=60 * 1024 * 1024),
        name="raise_and_add",
    )(lows, ups, base)


def kernel(
    groups, tensor, tile,
    slot_ref, id_ref, length_ref, x_ref, w_hbm, res_ref, down_hbm, up_hbm, low_hbm, up_in, base_hbm,
    w_ref, pair_out, pair_in, chip_out, chip_in, base, down_in, low_out, low_in, lows, down_pool, up_pool, down_out, up_out,
    w_sem, pool_sem, own_sem, out_sem, down_send, down_recv, up_send, up_recv,
    pair_send, pair_recv, chip_send, chip_recv, low_send, low_recv,
):
    me_t, me_r = lax.axis_index("tensor"), lax.axis_index("req")
    chips = tensor // 2
    chip, core = me_t // 2, lax.rem(me_t, 2)
    partner = chip * 2 + 1 - core
    width = res_ref.shape[1]
    tiles = width // tile
    rank = up_in.shape[1]
    blocks = []
    for step in range(1, chips + 1):
        there = lax.rem(chip + step, chips)
        blocks += [there * 2 + 1 - core, there * 2 + core]

    def far_first(k):
        half = (k + 1) // 2
        return lax.rem(me_r + groups // 2 + half - 2 * half * lax.rem(k, 2), groups)

    def weight_copy(i):
        column = pl.multiple_of(blocks[i] * width, width)
        return pltpu.make_async_copy(w_hbm.at[:, pl.ds(column, width)], w_ref.at[i], w_sem.at[i])

    def down_copy(peer, slot):
        return pltpu.make_async_remote_copy(
            src_ref=down_out.at[peer], dst_ref=down_in.at[slot],
            send_sem=down_send.at[peer], recv_sem=down_recv.at[slot],
            device_id=(me_t, peer), device_id_type=MESH)

    def up_copy(peer, slot):
        return pltpu.make_async_remote_copy(
            src_ref=up_out.at[peer], dst_ref=up_in.at[slot],
            send_sem=up_send.at[peer], recv_sem=up_recv.at[slot],
            device_id=(me_t, peer), device_id_type=MESH)

    def pair_copy(step, q):
        return pltpu.make_async_remote_copy(
            src_ref=pair_out.at[step, q], dst_ref=pair_in.at[step, q],
            send_sem=pair_send.at[step, q], recv_sem=pair_recv.at[step, q],
            device_id=(partner, me_r), device_id_type=MESH)

    def chip_copy(step, q):
        there = lax.rem(chip + step + 1, chips)
        return pltpu.make_async_remote_copy(
            src_ref=chip_out.at[step, q], dst_ref=chip_in.at[step, q],
            send_sem=chip_send.at[step, q], recv_sem=chip_recv.at[step, q],
            device_id=(there * 2 + core, me_r), device_id_type=MESH)

    def low_copy(step):
        return pltpu.make_async_remote_copy(
            src_ref=low_out, dst_ref=low_in.at[step - 1],
            send_sem=low_send.at[step - 1], recv_sem=low_recv.at[step - 1],
            device_id=(lax.rem(me_t + step, tensor), me_r), device_id_type=MESH)

    down_load = pltpu.make_async_copy(down_hbm, down_pool, pool_sem.at[0])
    up_load = pltpu.make_async_copy(up_hbm, up_pool, pool_sem.at[1])
    down_load.start()
    up_load.start()
    for i in range(2 * chips):
        weight_copy(i).start()
    own_down = pltpu.make_async_copy(down_out.at[me_r], down_in.at[me_r], own_sem.at[0])
    own_up = pltpu.make_async_copy(up_out.at[me_r], up_in.at[me_r], own_sem.at[1])

    barrier = pltpu.get_barrier_semaphore()

    @pl.loop(1, groups)
    def _(d):
        pl.semaphore_signal(
            barrier, inc=1, device_id=(me_t, lax.rem(me_r + d, groups)), device_id_type=MESH)

    for d in range(1, tensor):
        pl.semaphore_signal(
            barrier, inc=1, device_id=(lax.rem(me_t + d, tensor), me_r), device_id_type=MESH)
    pl.semaphore_wait(barrier, groups - 1 + tensor - 1)

    pool, requests = down_pool.shape[0], id_ref.shape[1]

    def wanted(group):
        row = jnp.int32(0)
        for r in range(requests):
            slot = slot_ref[id_ref[group, r]]
            row = row + jnp.where(slot // pool == me_r, slot % pool, 0)
        return row

    down_load.wait()

    @pl.loop(0, groups - 1)
    def _(k):
        peer = far_first(k)
        down_out[peer] = down_pool[wanted(peer)]
        down_copy(peer, me_r).start()

    up_load.wait()

    @pl.loop(0, groups - 1)
    def _(k):
        peer = far_first(k)
        up_out[peer] = up_pool[wanted(peer)]
        up_copy(peer, me_r).start()

    down_out[me_r] = down_pool[wanted(me_r)]
    up_out[me_r] = up_pool[wanted(me_r)]
    own_down.start()
    own_up.start()

    def product(i, q):
        columns = pl.ds(pl.multiple_of(q * tile, tile), tile)
        return jnp.dot(x_ref[...], w_ref[i, :, columns], preferred_element_type=F32)

    for step in range(chips):
        weight_copy(2 * step).wait()

        @pl.loop(0, tiles)
        def _(q):
            pair_out[step, q] = product(2 * step, q).astype(BF16)
            pair_copy(step, q).start()

        weight_copy(2 * step + 1).wait()

        @pl.loop(0, tiles)
        def _(q):
            mine = product(2 * step + 1, q)
            pair_copy(step, q).wait_recv()
            total = mine + pair_in[step, q].astype(F32)
            if step < chips - 1:
                chip_out[step, q] = total.astype(BF16)
                chip_copy(step, q).start()
            else:
                base[q] = total

    own_down.wait()

    @pl.loop(1, groups)
    def _(d):
        peer = lax.rem(me_r + d, groups)
        down_copy(peer, peer).wait_recv()

    span = 2 * rank
    positions = lax.broadcasted_iota(jnp.int32, low_out.shape, 0)
    owner = jnp.zeros(low_out.shape, jnp.int32)
    start = jnp.int32(0)
    for r in range(requests):
        owner = jnp.where(positions >= start, slot_ref[id_ref[me_r, r]] // pool, owner)
        start = start + length_ref[0, r]
    lane_owner = lax.broadcasted_iota(jnp.int32, (1, span), 1) // rank
    low = jnp.zeros(low_out.shape, F32)
    for pair in range(groups // 2):
        maps = down_in[2 * pair : 2 * pair + 2].reshape(span, x_ref.shape[1])
        value = lax.dot_general(
            x_ref[...], maps, (((1,), (1,)), ((), ())), preferred_element_type=F32)
        low = low + jnp.where(owner == 2 * pair + lane_owner, value, 0.0)
    low_out[...] = low.astype(BF16)
    for step in range(1, tensor):
        low_copy(step).start()
    low = low_out[...].astype(F32)
    for step in range(1, tensor):
        low_copy(step).wait_recv()
        low = low + low_in[step - 1].astype(F32)
    for pair in range(groups // 2):
        lows[:, pair * span : (pair + 1) * span] = jnp.where(
            owner == 2 * pair + lane_owner, low, 0.0).astype(BF16)
    low_write = pltpu.make_async_copy(lows, low_hbm, own_sem.at[2])
    low_write.start()

    def base_write(q):
        return pltpu.make_async_copy(base.at[q], base_hbm.at[q], out_sem.at[q])

    @pl.loop(0, tiles)
    def _(q):
        columns = pl.ds(pl.multiple_of(q * tile, tile), tile)
        total = base[q] + res_ref[:, columns].astype(F32)
        for step in range(chips - 1):
            chip_copy(step, q).wait_recv()
            total = total + chip_in[step, q].astype(F32)
        base[q] = total
        base_write(q).start()

    own_up.wait()

    @pl.loop(1, groups)
    def _(d):
        peer = lax.rem(me_r + d, groups)
        up_copy(peer, peer).wait_recv()

    low_write.wait()

    @pl.loop(0, tiles)
    def _(q):
        base_write(q).wait()

    @pl.loop(1, groups)
    def _(d):
        peer = lax.rem(me_r + d, groups)
        down_copy(peer, me_r).wait_send()
        up_copy(peer, me_r).wait_send()

    for step in range(chips):
        @pl.loop(0, tiles)
        def _(q):
            pair_copy(step, q).wait_send()
            if step < chips - 1:
                chip_copy(step, q).wait_send()

    for step in range(1, tensor):
        low_copy(step).wait_send()


def per_device(
    attention_output,
    residual,
    projection_weight,
    adapter_down_maps,
    adapter_up_maps,
    adapter_pool_slot,
    request_adapter_id,
    request_token_length,
):
    groups, tensor = lax.axis_size("req"), lax.axis_size("tensor")
    tokens, depth = attention_output.shape
    width = residual.shape[1]
    pool, _, rank = adapter_down_maps.shape
    tile = min(512, width)
    tiles = width // tile
    chips = tensor // 2
    far = max(chips - 1, 1)
    smem = pl.BlockSpec(memory_space=pltpu.SMEM)
    vmem = pl.BlockSpec(memory_space=pltpu.VMEM)
    hbm = pl.BlockSpec(memory_space=pl.ANY)
    dma = pltpu.SemaphoreType.DMA
    flops = 2 * tokens * depth * width * tensor
    lows, ups, base = pl.pallas_call(
        functools.partial(kernel, groups, tensor, tile),
        out_shape=[
            jax.ShapeDtypeStruct((tokens, groups * rank), BF16),
            jax.ShapeDtypeStruct((groups, rank, width), BF16),
            jax.ShapeDtypeStruct((tiles, tokens, tile), F32),
        ],
        in_specs=[smem, smem, smem, vmem, hbm, vmem, hbm, hbm],
        out_specs=[hbm, hbm, hbm],
        scratch_shapes=[
            pltpu.VMEM((tensor, depth, width), BF16),
            pltpu.VMEM((chips, tiles, tokens, tile), BF16),
            pltpu.VMEM((chips, tiles, tokens, tile), BF16),
            pltpu.VMEM((far, tiles, tokens, tile), BF16),
            pltpu.VMEM((far, tiles, tokens, tile), BF16),
            pltpu.VMEM((tiles, tokens, tile), F32),
            pltpu.VMEM((groups, rank, depth), BF16),
            pltpu.VMEM((tokens, 2 * rank), BF16),
            pltpu.VMEM((tensor - 1, tokens, 2 * rank), BF16),
            pltpu.VMEM((tokens, groups * rank), BF16),
            pltpu.VMEM((pool, rank, depth), BF16),
            pltpu.VMEM((pool, rank, width), BF16),
            pltpu.VMEM((groups, rank, depth), BF16),
            pltpu.VMEM((groups, rank, width), BF16),
            dma((tensor,)),
            dma((2,)),
            dma((3,)),
            dma((tiles,)),
            dma((groups,)),
            dma((groups,)),
            dma((groups,)),
            dma((groups,)),
            dma((chips, tiles)),
            dma((chips, tiles)),
            dma((far, tiles)),
            dma((far, tiles)),
            dma((tensor - 1,)),
            dma((tensor - 1,)),
        ],
        compiler_params=pltpu.CompilerParams(
            collective_id=0, has_side_effects=True, vmem_limit_bytes=60 * 1024 * 1024
        ),
        cost_estimate=pl.CostEstimate(
            flops=flops, bytes_accessed=2 * depth * width * tensor, transcendentals=0
        ),
        name="project_and_adapt",
    )(
        adapter_pool_slot, request_adapter_id, request_token_length,
        attention_output, projection_weight, residual,
        adapter_down_maps.transpose(0, 2, 1), adapter_up_maps,
    )
    return finish(lows, ups, base)


def solution(mesh):
    in_specs = (
        P("req", "tensor"),
        P("req", "tensor"),
        P("tensor", None),
        P("req", "tensor", None),
        P("req", None, "tensor"),
        P(),
        P(),
        P("req", None),
    )
    out_specs = P("req", "tensor")
    return jax.shard_map(
        per_device, mesh=mesh, in_specs=in_specs, out_specs=out_specs, check_vma=False
    )
```
